32 devices in a mesh: dp: 8 (over z, x), ctx: 4 (over y, core).
Axes of the slice: x: 2, y: 2, z: 4, core: 2. Of those that a mesh axis runs over, the one named last changes fastest.
Arguments:
- tokens: bfloat16 [8, 4096, 768], P('dp', 'ctx'), may hold values from -6 to 6
- cotangent: bfloat16 [8, 4096, 768], P('dp', 'ctx'), may hold values from -6 to 6
- in_master: float32 [768, 3352], P('ctx'), may hold values from -0.21875 to 0.21875
- in_moment: float32 [768, 3352], P('ctx'), may hold values from -0.00036621094 to 0.00036621094
- in_second: float32 [768, 3352], P('ctx'), may hold values from 2.6558167e-10 to 1.0623267e-09
- out_master: float32 [1536, 768], P('ctx'), may hold values from -0.15625 to 0.15625
- out_moment: float32 [1536, 768], P('ctx'), may hold values from -0.00036621094 to 0.00036621094
- out_second: float32 [1536, 768], P('ctx'), may hold values from 2.6558167e-10 to 1.0623267e-09
- vec_master: float32 [11336], P('ctx'), may hold values from -7 to 3
- vec_moment: float32 [11336], P('ctx'), may hold values from -0.0014648438 to 0.0014648438
- vec_second: float32 [11336], P('ctx'), may hold values from 4.2493067e-09 to 1.6997227e-08
Outputs:
- mixed: bfloat16 [8, 4096, 768], P('dp', 'ctx')
- tokens_grad: float32 [8, 4096, 768], P('dp', 'ctx')
- in_first: float32 [768, 3352], P('ctx')
- in_square: float32 [768, 3352], P('ctx')
- in_updated: float32 [768, 3352], P('ctx')
- out_first: float32 [1536, 768], P('ctx')
- out_square: float32 [1536, 768], P('ctx')
- out_updated: float32 [1536, 768], P('ctx')
- vec_first: float32 [11336], P('ctx')
- vec_square: float32 [11336], P('ctx')
- vec_updated: float32 [11336], P('ctx')
- grad_norm: float32 [], replicated
The draws below stay inside these ranges and needn't reach their ends.
All inputs are finite; a program needn't handle non-finite values.
Results may differ from the reference program's by a relative error of at most 0.012.
The reference program's roundings to bfloat16 on the way (of `normed` and `gated_norm`) count: a program that leaves them out, or rounds other values in their place, can miss the bound.
Values may be sent and summed in bfloat16 or wider, within the bound.
A program may use at most 256 MiB of HBM per device.

```python
import math
import jax
import jax.numpy as jnp
from jax import lax

D = 768
HEADS = 24
HEADDIM = 64
STATE = 128
CONV = 4
SPAN = 256
STEP = 10
INNER = 1536
CONVCH = 1792
PROJ = 3352
NVEC = 11336
NPARAM = 3765320
SEQS = 8
LEN = 4096


def draw_vec_master(key, part):
    key = jax.random.fold_in(key, 7)
    keys = jax.random.split(key, 7)
    growth = 3.0
    rate_low = -4.0
    rate_high = 0.5
    bias_low = -7.0
    bias_high = -2.3
    norm_gain = jnp.exp(jnp.log(growth) * (jnp.arange(D).astype(jnp.float32) / D - 0.5)) * jax.random.uniform(keys[0], (D,), jnp.float32, 0.7, 1.3)
    gate_gain = jnp.exp(jnp.log(growth) * (jnp.arange(INNER).astype(jnp.float32) / INNER - 0.5)) * jax.random.uniform(keys[1], (INNER,), jnp.float32, 0.7, 1.3)
    taps = jax.random.uniform(keys[2], (CONVCH * CONV,), jnp.float32, -0.9, 0.9)
    conv_bias = jax.random.uniform(keys[3], (CONVCH,), jnp.float32, -0.5, 0.5)
    step_bias = jax.random.uniform(keys[4], (HEADS,), jnp.float32, bias_low, bias_high)
    log_rate = jax.random.uniform(keys[5], (HEADS,), jnp.float32, rate_low, rate_high)
    skip_gain = jax.random.uniform(keys[6], (HEADS,), jnp.float32, 0.5, 1.5)
    return jnp.concatenate([norm_gain, gate_gain, taps, conv_bias, step_bias, log_rate, skip_gain]).astype(jnp.float32)


def shard_levels(rng, dims, shards, least, largest):
    def one(dim, parts):
        heights = jax.random.uniform(jax.random.fold_in(jax.random.fold_in(rng, 6), dim), (parts,), jnp.float32, least / len(shards), largest / len(shards))
        return jnp.repeat(jnp.exp(heights), dims[dim] // parts).reshape((-1,) + (1,) * (len(dims) - dim - 1))

    loudness = one(*shards[0])
    for cut in shards[1:]:
        loudness = loudness * one(*cut)
    return loudness


def bell_draw(key, dims, spread, most, shards=(), kind=jnp.bfloat16):
    loudness = shard_levels(key, dims, shards, -0.22, 0.18) if shards else 1.0
    entries = jax.random.normal(key, dims, jnp.float32) * spread * loudness
    return jnp.minimum(jnp.maximum(entries, -most), most).astype(kind)


def setup_inputs(seed: int = 0) -> dict:
    arg_keys = jax.random.split(jax.random.key(seed), 12)
    return {
        "tokens": bell_draw(arg_keys[0], (SEQS, LEN, D), 1.0, 6.0, ((0, 8), (1, 4))),
        "cotangent": bell_draw(arg_keys[1], (SEQS, LEN, D), 1.0, 6.0, ((0, 8), (1, 4))),
        "in_master": bell_draw(arg_keys[2], (D, PROJ), D ** -0.5, 0.21875, ((0, 4),), jnp.float32),
        "in_moment": bell_draw(arg_keys[3], (D, PROJ), (0.111 / NPARAM ** 0.5), 0.00036621094, ((0, 4),), jnp.float32),
        "in_second": jnp.clip(jnp.exp(math.log(1.0623266710751977e-09) - 1.3862944 * jax.random.uniform(arg_keys[4], (D, PROJ), jnp.float32) ** shard_levels(arg_keys[4], (D, PROJ), ((0, 4),), -0.2, 0.2)), 2.6558166776879943e-10, 1.0623266710751977e-09),
        "out_master": bell_draw(arg_keys[5], (INNER, D), INNER ** -0.5, 0.15625, ((0, 4),), jnp.float32),
        "out_moment": bell_draw(arg_keys[6], (INNER, D), (0.111 / NPARAM ** 0.5), 0.00036621094, ((0, 4),), jnp.float32),
        "out_second": jnp.clip(jnp.exp(math.log(1.0623266710751977e-09) - 1.3862944 * jax.random.uniform(arg_keys[7], (INNER, D), jnp.float32) ** shard_levels(arg_keys[7], (INNER, D), ((0, 4),), -0.2, 0.2)), 2.6558166776879943e-10, 1.0623266710751977e-09),
        "vec_master": draw_vec_master(jax.random.fold_in(arg_keys[11], 71), 0),
        "vec_moment": bell_draw(arg_keys[9], (NVEC,), (0.444 / NPARAM ** 0.5), 0.0014648438, ((0, 4),), jnp.float32),
        "vec_second": jnp.clip(jnp.exp(math.log(1.6997226737203164e-08) - 1.3862944 * jax.random.uniform(arg_keys[10], (NVEC,), jnp.float32) ** shard_levels(arg_keys[10], (NVEC,), ((0, 4),), -0.2, 0.2)), 4.249306684300791e-09, 1.6997226737203164e-08),
    }


@jax.custom_vjp
def low(v):
    return lax.optimization_barrier(v.astype(jnp.bfloat16)).astype(jnp.float32)

@jax.custom_vjp
def low_back(v):
    return v

def low_keep(v):
    return (low(v), None)

def low_pass(kept, grad):
    return (grad,)

def back_keep(v):
    return (v, None)

def back_low(kept, grad):
    return (low(grad),)
low.defvjp(low_keep, low_pass)
low_back.defvjp(back_keep, back_low)
EPS_NORM = 1e-05
BETA_ONE = 0.9
BETA_TWO = 0.999
ADAM_EPS = 1e-08
HIGH = lax.Precision.HIGHEST

def unpack(packed):
    offset = 0
    pieces = []
    for count in (D, INNER, CONVCH * CONV, CONVCH, HEADS, HEADS, HEADS):
        pieces.append(packed[offset:offset + count])
        offset = offset + count
    norm_gain, gate_gain, taps, conv_bias, step_bias, log_rate, skip_gain = pieces
    return (norm_gain, gate_gain, taps.reshape(CONVCH, CONV), conv_bias, step_bias, log_rate, skip_gain)

def rms_scale(values, gain):
    return values * lax.rsqrt(lax.optimization_barrier(jnp.mean(values * values, axis=-1, keepdims=True)) + EPS_NORM) * gain

def prepare(projected, previous, taps, conv_bias, step_bias, log_rate):
    gate = projected[:, :INNER]
    conv_in = projected[:, INNER:INNER + CONVCH]
    step_raw = projected[:, INNER + CONVCH:]
    count = conv_in.shape[0]
    padded = jnp.concatenate([previous, conv_in], axis=0)
    total = conv_bias + jnp.zeros_like(conv_in)
    for shift_k in range(CONV):
        total = total + padded[shift_k:shift_k + count] * taps[:, shift_k]
    conv_out = jax.nn.silu(total)
    values = conv_out[:, :INNER].reshape(count, HEADS, HEADDIM)
    bmat = conv_out[:, INNER:INNER + STATE]
    cmat = conv_out[:, INNER + STATE:]
    step = jax.nn.softplus(step_raw + step_bias)
    logdec = -step * jnp.exp(log_rate)
    scaled = values * step[:, :, None]
    return (gate, values, scaled, logdec, bmat, cmat)

def span_step(carried, pieces):
    scaled, logdec, bmat, cmat = pieces
    cumul = jnp.cumsum(logdec, axis=0)
    places = jnp.arange(scaled.shape[0])
    lower = (places[:, None] >= places[None, :])[:, :, None]
    gaps = jnp.where(lower, cumul[:, None, :] - cumul[None, :, :], 0.0)
    decays = jnp.where(lower, jnp.exp(gaps), 0.0)
    inner = jnp.dot(cmat, bmat.T, precision=HIGH)
    outputs = jnp.einsum('tsh,shp->thp', inner[:, :, None] * decays, scaled, precision=HIGH)
    outputs = outputs + jnp.einsum('tn,th,hpn->thp', cmat, jnp.exp(cumul), carried, precision=HIGH)
    tails = jnp.exp(cumul[-1][None, :] - cumul)
    carried = jnp.exp(cumul[-1])[:, None, None] * carried + jnp.einsum('sh,shp,sn->hpn', tails, scaled, bmat, precision=HIGH)
    return (carried, outputs)

def recurrence(scaled, logdec, bmat, cmat):
    count = scaled.shape[0] // SPAN
    pieces = (scaled.reshape(count, SPAN, HEADS, HEADDIM), logdec.reshape(count, SPAN, HEADS), bmat.reshape(count, SPAN, STATE), cmat.reshape(count, SPAN, STATE))
    start = jnp.zeros((HEADS, HEADDIM, STATE), jnp.float32)
    final, outputs = lax.scan(jax.checkpoint(span_step), start, pieces)
    return outputs.reshape(-1, HEADS, HEADDIM)

def forward_sequence(sequence, w_in, w_out, packed):
    norm_gain, gate_gain, taps, conv_bias, step_bias, log_rate, skip_gain = unpack(packed)
    normed = low(rms_scale(sequence, norm_gain))
    projected = low_back(jnp.dot(normed, w_in, precision=HIGH))
    previous = jnp.zeros((CONV - 1, CONVCH), jnp.float32)
    gate, values, scaled, logdec, bmat, cmat = prepare(projected, previous, taps, conv_bias, step_bias, log_rate)
    ssd = recurrence(scaled, logdec, bmat, cmat)
    joined = (ssd + skip_gain[:, None] * values).reshape(-1, INNER)
    gated_norm = low(rms_scale(joined * jax.nn.silu(gate), gate_gain))
    return sequence + jnp.dot(gated_norm, w_out, precision=HIGH)

def adamw(master, moment, second, grad, rate, decay):
    first = BETA_ONE * moment + (1.0 - BETA_ONE) * grad
    square = BETA_TWO * second + (1.0 - BETA_TWO) * grad * grad
    ahead = first / (1.0 - BETA_ONE ** STEP)
    scale = square / (1.0 - BETA_TWO ** STEP)
    updated = master - rate * (ahead / (jnp.sqrt(scale) + ADAM_EPS) + decay * master)
    return (first, square, updated)

def reference(tokens, cotangent, in_master, in_moment, in_second, out_master, out_moment, out_second, vec_master, vec_moment, vec_second):
    w_in = in_master.astype(jnp.bfloat16).astype(jnp.float32)
    w_out = out_master.astype(jnp.bfloat16).astype(jnp.float32)
    packed = vec_master.astype(jnp.bfloat16).astype(jnp.float32)

    def per_sequence(carry, pair):
        sequence, seq_cot = pair
        output, pullback = jax.vjp(forward_sequence, sequence.astype(jnp.float32), w_in, w_out, packed)
        d_seq, g_in, g_out, g_vec = pullback(seq_cot.astype(jnp.float32))
        carry = (carry[0] + g_in, carry[1] + g_out, carry[2] + g_vec)
        return (carry, (output.astype(jnp.bfloat16), d_seq))
    start = (jnp.zeros((D, PROJ), jnp.float32), jnp.zeros((INNER, D), jnp.float32), jnp.zeros((NVEC,), jnp.float32))
    (g_in, g_out, g_vec), (mixed, tokens_grad) = lax.scan(per_sequence, start, (tokens, cotangent))
    grad_norm = jnp.sqrt(jnp.sum(g_in * g_in) + jnp.sum(g_out * g_out) + jnp.sum(g_vec * g_vec))
    factor = 1.0 / jnp.maximum(grad_norm, 1.0)
    in_first, in_square, in_updated = adamw(in_master, in_moment, in_second, g_in * factor, 0.05, 0.01)
    out_first, out_square, out_updated = adamw(out_master, out_moment, out_second, g_out * factor, 0.05, 0.01)
    vec_first, vec_square, vec_updated = adamw(vec_master, vec_moment, vec_second, g_vec * factor, 0.5, 0.0)
    return (mixed, tokens_grad, in_first, in_square, in_updated, out_first, out_square, out_updated, vec_first, vec_square, vec_updated, grad_norm)
```

```python
import jax
import jax.numpy as jnp
from jax import lax
from jax.experimental import pallas as pl
from jax.experimental.pallas import tpu as pltpu
from jax.sharding import PartitionSpec as P

D = 768
HEADS = 24
HEADDIM = 64
STATE = 128
CONV = 4
SPAN = 256
STEP = 10
INNER = 1536
CONVCH = 1792
LANES = 128
REST = CONVCH + LANES
PAIRS = HEADS // 2

EPS_NORM = 1e-05
BETA_ONE = 0.9
BETA_TWO = 0.999
ADAM_EPS = 1e-08
HIGH = lax.Precision.HIGHEST
LOW = jnp.bfloat16
F32 = jnp.float32


def mul(a, b, ca=1, cb=0):
    return lax.dot_general(
        a.astype(LOW), b.astype(LOW), (((ca,), (cb,)), ((), ())), preferred_element_type=F32
    )


def spread(v, expand):
    top = v.astype(LOW)
    rest = (v - top.astype(F32)).astype(LOW)
    return mul(top, expand) + mul(rest, expand)


def lower_mask():
    rows = lax.broadcasted_iota(jnp.int32, (SPAN, SPAN), 0)
    cols = lax.broadcasted_iota(jnp.int32, (SPAN, SPAN), 1)
    return rows >= cols


def softplus(z):
    return jnp.maximum(z, 0.0) + jnp.log1p(jnp.exp(-jnp.abs(z)))


def conv_total(ext, taps):
    total = taps[4:5, :] + ext[5 : 5 + SPAN] * taps[0:1, :]
    for k in range(1, CONV):
        total = total + ext[5 + k : 5 + k + SPAN] * taps[k : k + 1, :]
    return total


def scan_kernel(
    rest, prev, taps, heads, expand, y, xbc, cumtot, starts, runs, final, state, tail, run
):
    i = pl.program_id(0)

    @pl.when(i == 0)
    def _():
        state[...] = jnp.zeros_like(state)
        run[...] = jnp.zeros_like(run)
        tail[...] = prev[...]

    ext = jnp.concatenate([tail[...], rest[:, :CONVCH]], axis=0)
    total = conv_total(ext, taps)
    tail[...] = rest[SPAN - 8 :, :CONVCH]
    out = total * jax.nn.sigmoid(total)
    xbc[...] = out.astype(LOW)
    x = out[:, :INNER]
    bmat = out[:, INNER : INNER + STATE].astype(LOW)
    cmat = out[:, INNER + STATE :].astype(LOW)
    step = softplus(rest[:, CONVCH:] + heads[0:1, :])
    logdec = -step * heads[1:2, :]
    lower = lower_mask()
    cum = jnp.dot(
        jnp.where(lower, 1.0, 0.0).astype(F32), logdec, precision=HIGH, preferred_element_type=F32
    )
    cum_t = cum.T
    last = cum[SPAN - 1 :, :]
    before = run[...]
    cumtot[...] = cum + before[0:1, :]
    runs[0] = before
    run[...] = before + last
    e = expand[...]
    xs = (x * spread(step, e)).astype(LOW)
    own = mul(bmat, x * spread(step * jnp.exp(last - cum), e), 0, 0)
    held = state[...]
    starts[0] = held
    inner = mul(cmat, bmat, 1, 1)
    lane = lax.broadcasted_iota(jnp.int32, (SPAN, 2 * HEADDIM), 1) < HEADDIM
    carried = spread(jnp.exp(cum), e) * mul(cmat, held)
    zero = jnp.zeros((), LOW)
    for p in range(PAIRS):
        at = slice(p * 2 * HEADDIM, (p + 1) * 2 * HEADDIM)
        both = carried[:, at]
        for j in range(2):
            h = 2 * p + j
            gap = cum[:, h : h + 1] - cum_t[h : h + 1, :]
            m = (jnp.where(lower, jnp.exp(gap), 0.0) * inner).astype(LOW)
            mine = lane if j == 0 else jnp.logical_not(lane)
            both = both + mul(m, jnp.where(mine, xs[:, at], zero))
        y[:, at] = both
    new = held * spread(jnp.exp(jnp.broadcast_to(last, (8, LANES))), e)[0:1, :] + own
    state[...] = new
    final[...] = new


def gate_kernel(
    y, xbc, gate, cumtot, entry, cot, tokens, w_out, rows, expand,
    gated, mixed, dgate, dssd, acc, dentry,
):
    i = pl.program_id(0)

    @pl.when(i == 0)
    def _():
        acc[...] = jnp.zeros_like(acc)
        dentry[...] = jnp.zeros_like(dentry)

    x = xbc[:, :INNER].astype(F32)
    cmat = xbc[:, INNER + STATE :]
    grown = spread(jnp.exp(cumtot[...]), expand[...])
    gain = rows[0:1, :]
    joined = y[...] + grown * mul(cmat, entry[...]) + rows[1:2, :] * x
    g = gate[...]
    sg = jax.nn.sigmoid(g)
    s = g * sg
    u = joined * s
    r = lax.rsqrt(jnp.mean(u * u, axis=1, keepdims=True) + EPS_NORM)
    n = u * r
    low = (n * gain).astype(LOW)
    gated[...] = low
    w = w_out[...]
    mixed[...] = (tokens[...].astype(F32) + mul(low, w)).astype(LOW)
    dgn = mul(cot[...], w, 1, 1)
    acc[0:1, :] += jnp.sum(dgn * n, axis=0, keepdims=True)
    dn = dgn * gain
    du = r * (dn - n * jnp.mean(dn * n, axis=1, keepdims=True))
    dj = du * s
    dgate[...] = (du * joined * (sg * (1.0 + g * (1.0 - sg)))).astype(LOW)
    dssd[...] = dj.astype(LOW)
    acc[1:2, :] += jnp.sum(dj * x, axis=0, keepdims=True)
    dentry[...] += mul(cmat, grown * dj, 0, 0)


def back_kernel(
    rest, ahead, prev, taps, heads, expand, dssd, starts, runs, entry, d_exit, skip,
    d_rest, last8, d_prev, acc, hacc, adj, nxt, dxs_ref, cb_ref,
):
    i = pl.program_id(0)
    first_span = i == pl.num_programs(0) - 1

    @pl.when(i == 0)
    def _():
        adj[...] = d_exit[...]
        nxt[...] = jnp.zeros_like(nxt)
        acc[...] = jnp.zeros_like(acc)
        hacc[...] = jnp.zeros_like(hacc)

    e = expand[...]
    ext = jnp.concatenate(
        [jnp.where(first_span, prev[...], ahead[:, :CONVCH]), rest[:, :CONVCH]], axis=0
    )
    total = conv_total(ext, taps)
    sig = jax.nn.sigmoid(total)
    out = total * sig
    x = out[:, :INNER]
    bmat = out[:, INNER : INNER + STATE].astype(LOW)
    cmat = out[:, INNER + STATE :].astype(LOW)
    z = rest[:, CONVCH:] + heads[0:1, :]
    step = softplus(z)
    logdec = -step * heads[1:2, :]
    lower = lower_mask()
    tri = jnp.where(lower, 1.0, 0.0).astype(F32)
    cum = jnp.dot(tri, logdec, precision=HIGH, preferred_element_type=F32)
    cum_t = cum.T
    last = cum[SPAN - 1 :, :]
    dy = dssd[...]
    step_e = spread(step, e)
    xs32 = x * step_e
    xs = xs32.astype(LOW)
    g = adj[...]
    span_decay = spread(jnp.exp(jnp.broadcast_to(last, (8, LANES))), e)[0:1, :]
    start = starts[0] + spread(jnp.exp(runs[0]), e)[0:1, :] * entry[...]
    grown = spread(jnp.exp(cum), e)
    tails_e = spread(jnp.exp(last - cum), e)
    dyg = grown * dy.astype(F32)
    from_start = (dyg * mul(cmat, start)).astype(LOW)
    dxs_tail = tails_e * mul(bmat, g)
    to_tail = (xs32 * dxs_tail).astype(LOW)
    grow_sum = mul(from_start, e, 1, 1)
    tail_sum = mul(to_tail, e, 1, 1)
    ends = span_decay * jnp.sum(start * g, axis=0, keepdims=True)
    end_sum = mul(jnp.broadcast_to(ends, (8, INNER)), e, 1, 1)[0:1, :]
    end_sum = end_sum + jnp.sum(tail_sum, axis=0, keepdims=True)
    dc = mul(dyg, start, 1, 1)
    db = mul(xs32 * tails_e, g, 1, 1)
    adj[...] = span_decay * g + mul(cmat, dyg, 0, 0)
    inner = mul(cmat, bmat, 1, 1)
    lane = lax.broadcasted_iota(jnp.int32, (SPAN, 2 * HEADDIM), 1) < HEADDIM
    column = lax.broadcasted_iota(jnp.int32, (SPAN, LANES), 1)
    zero = jnp.zeros((), LOW)
    cb_ref[...] = jnp.zeros_like(cb_ref)
    dcum = grow_sum - tail_sum
    for p in range(PAIRS):
        at = slice(p * 2 * HEADDIM, (p + 1) * 2 * HEADDIM)
        both = dxs_tail[:, at]
        for j in range(2):
            h = 2 * p + j
            gap = cum[:, h : h + 1] - cum_t[h : h + 1, :]
            decay = jnp.where(lower, jnp.exp(gap), 0.0)
            mine = lane if j == 0 else jnp.logical_not(lane)
            part = jnp.where(mine, dy[:, at], zero)
            back = mul(part, xs[:, at], 1, 1) * decay
            cb_ref[...] += back
            both = both + mul(decay * inner, part, 0, 0)
            pull = (back * inner).astype(LOW)
            unit = jnp.where(column == h, 1.0, 0.0).astype(LOW)
            dcum = dcum + (mul(pull, unit) - mul(pull, unit, 0, 0))
        dxs_ref[:, at] = both
    d_inner = cb_ref[...]
    dc = dc + mul(d_inner, bmat)
    db = db + mul(d_inner, cmat, 0, 0)
    dxs = dxs_ref[...]
    d_logdec = end_sum + lax.dot_general(
        tri, dcum, (((0,), (0,)), ((), ())), precision=HIGH, preferred_element_type=F32
    )
    d_step = mul(x * dxs, e, 1, 1) - d_logdec * heads[1:2, :]
    real = column < HEADS
    d_raw = jnp.where(real, d_step * jax.nn.sigmoid(z), 0.0)
    hacc[0:1, :] += jnp.sum(d_raw, axis=0, keepdims=True)
    hacc[1:2, :] += jnp.sum(d_logdec * logdec, axis=0, keepdims=True)
    dx = step_e * dxs + skip[1:2, :] * dy.astype(F32)
    d_out = jnp.concatenate([dx, db, dc], axis=1)
    dt = d_out * (sig * (1.0 + total * (1.0 - sig)))
    for k in range(CONV):
        acc[k : k + 1, :] += jnp.sum(dt * ext[5 + k : 5 + k + SPAN], axis=0, keepdims=True)
    acc[4:5, :] += jnp.sum(dt, axis=0, keepdims=True)
    later = jnp.concatenate([dt, nxt[...]], axis=0)
    d_in = later[:SPAN] * taps[3:4, :]
    for k in range(CONV - 1):
        d_in = d_in + later[3 - k : 3 - k + SPAN] * taps[k : k + 1, :]
    d_rest[:, :CONVCH] = d_in.astype(LOW)
    d_rest[:, CONVCH:] = d_raw.astype(LOW)

    @pl.when(i == 0)
    def _():
        last8[...] = d_in[SPAN - 8 :]

    front = dt[:8]
    nxt[...] = front
    edge = jnp.concatenate([jnp.zeros_like(front), front, jnp.zeros_like(front)], axis=0)
    d_before = edge[:8] * taps[3:4, :]
    for k in range(CONV - 1):
        d_before = d_before + edge[3 - k : 11 - k] * taps[k : k + 1, :]
    d_prev[...] = d_before


def whole(*shape):
    return pl.BlockSpec(shape, lambda i: (0,) * len(shape))


def span(width):
    return pl.BlockSpec((SPAN, width), lambda i: (i, 0))


def params():
    return pltpu.CompilerParams(vmem_limit_bytes=56 * 1024 * 1024)


def shape(dims, kind=F32):
    return jax.ShapeDtypeStruct(dims, kind)


def run_scan(rest, prev, taps, heads, expand):
    rows = rest.shape[0]
    n = rows // SPAN
    return pl.pallas_call(
        scan_kernel,
        grid=(n,),
        in_specs=[
            span(REST), whole(8, CONVCH), whole(8, CONVCH), whole(8, LANES), whole(LANES, INNER),
        ],
        out_specs=[
            span(INNER), span(CONVCH), span(LANES),
            pl.BlockSpec((1, STATE, INNER), lambda i: (i, 0, 0)),
            pl.BlockSpec((1, 8, LANES), lambda i: (i, 0, 0)),
            whole(STATE, INNER),
        ],
        out_shape=[
            shape((rows, INNER)), shape((rows, CONVCH), LOW), shape((rows, LANES)),
            shape((n, STATE, INNER)), shape((n, 8, LANES)), shape((STATE, INNER)),
        ],
        scratch_shapes=[
            pltpu.VMEM((STATE, INNER), F32), pltpu.VMEM((8, CONVCH), F32),
            pltpu.VMEM((8, LANES), F32),
        ],
        compiler_params=params(),
        name="span_scan",
    )(rest, prev, taps, heads, expand)


def run_gate(y, xbc, gate, cumtot, entry, cot, tokens, w_out, rows8, expand):
    rows = y.shape[0]
    return pl.pallas_call(
        gate_kernel,
        grid=(rows // SPAN,),
        in_specs=[
            span(INNER), span(CONVCH), span(INNER), span(LANES), whole(STATE, INNER),
            span(D), span(D), whole(INNER, D), whole(8, INNER), whole(LANES, INNER),
        ],
        out_specs=[
            span(INNER), span(D), span(INNER), span(INNER), whole(8, INNER), whole(STATE, INNER),
        ],
        out_shape=[
            shape((rows, INNER), LOW), shape((rows, D), LOW), shape((rows, INNER), LOW),
            shape((rows, INNER), LOW), shape((8, INNER)), shape((STATE, INNER)),
        ],
        compiler_params=params(),
        name="gate_and_back",
    )(y, xbc, gate, cumtot, entry, cot, tokens, w_out, rows8, expand)


def run_back(rest, prev, taps, heads, expand, dssd, starts, runs, entry, d_exit, rows8):
    rows = rest.shape[0]
    n = rows // SPAN
    flip = lambda i: (n - 1 - i, 0)
    flip3 = lambda i: (n - 1 - i, 0, 0)
    edge = SPAN // 8
    return pl.pallas_call(
        back_kernel,
        grid=(n,),
        in_specs=[
            pl.BlockSpec((SPAN, REST), flip),
            pl.BlockSpec((8, REST), lambda i: (jnp.maximum((n - 1 - i) * edge - 1, 0), 0)),
            whole(8, CONVCH), whole(8, CONVCH), whole(8, LANES), whole(LANES, INNER),
            pl.BlockSpec((SPAN, INNER), flip),
            pl.BlockSpec((1, STATE, INNER), flip3),
            pl.BlockSpec((1, 8, LANES), flip3),
            whole(STATE, INNER), whole(STATE, INNER), whole(8, INNER),
        ],
        out_specs=[
            pl.BlockSpec((SPAN, REST), flip),
            whole(8, CONVCH), whole(8, CONVCH), whole(8, CONVCH), whole(8, LANES),
        ],
        out_shape=[
            shape((rows, REST), LOW), shape((8, CONVCH)), shape((8, CONVCH)),
            shape((8, CONVCH)), shape((8, LANES)),
        ],
        scratch_shapes=[
            pltpu.VMEM((STATE, INNER), F32), pltpu.VMEM((8, CONVCH), F32),
            pltpu.VMEM((SPAN, INNER), F32), pltpu.VMEM((SPAN, SPAN), F32),
        ],
        compiler_params=params(),
        name="span_back",
    )(rest, rest, prev, taps, heads, expand, dssd, starts, runs, entry, d_exit, rows8)


def unpack(packed):
    offset = 0
    pieces = []
    for count in (D, INNER, CONVCH * CONV, CONVCH, HEADS, HEADS, HEADS):
        pieces.append(packed[offset : offset + count])
        offset = offset + count
    return pieces


def rms_scale(values, gain):
    return values * lax.rsqrt(jnp.mean(values * values, axis=-1, keepdims=True) + EPS_NORM) * gain


def shifted(block, axis, distance):
    devices = range(lax.axis_size(axis))
    route = [(i - distance, i) for i in devices if i - distance in devices]
    return lax.ppermute(block, axis, route)


def adamw(master, moment, second, grad, rate, decay):
    first = BETA_ONE * moment + (1.0 - BETA_ONE) * grad
    square = BETA_TWO * second + (1.0 - BETA_TWO) * grad * grad
    ahead = first / (1.0 - BETA_ONE**STEP)
    scale = square / (1.0 - BETA_TWO**STEP)
    updated = master - rate * (ahead / (jnp.sqrt(scale) + ADAM_EPS) + decay * master)
    return (first, square, updated)


def gathered(shard):
    return lax.all_gather(shard.astype(LOW), "ctx", axis=0, tiled=True)


def summed(grad):
    return lax.psum(
        lax.psum_scatter(grad.astype(LOW), "ctx", scatter_dimension=0, tiled=True), "dp"
    ).astype(F32)


def stack8(*rows):
    out = jnp.stack(rows)
    return jnp.pad(out, ((0, 8 - out.shape[0]), (0, 0)))


def one_sequence(tokens, cotangent, w_gate, w_rest, w_out, packed):
    norm_gain, gate_gain, taps, conv_bias, step_bias, log_rate, skip_gain = unpack(packed)
    place = lax.axis_index("ctx")
    count = lax.axis_size("ctx")
    block = tokens.shape[0]
    flat = tokens.astype(F32)
    normed, front_pull = jax.vjp(rms_scale, flat, norm_gain)
    normed_low = normed.astype(LOW)
    rest = jnp.dot(normed_low, w_rest, preferred_element_type=F32)
    prev = shifted(rest[block - 8 :, :CONVCH], "ctx", 1)
    gate = jnp.dot(normed_low, w_gate, preferred_element_type=F32)
    taps8 = jnp.pad(
        jnp.concatenate([taps.reshape(CONVCH, CONV).T, conv_bias[None]]), ((0, 3), (0, 0))
    )
    heads8 = jnp.pad(stack8(step_bias, jnp.exp(log_rate)), ((0, 0), (0, LANES - HEADS)))
    rows8 = stack8(gate_gain, jnp.repeat(skip_gain, HEADDIM))
    expand = (jnp.arange(LANES)[:, None] == jnp.arange(INNER)[None, :] // HEADDIM).astype(LOW)
    y, xbc, cumtot, starts, runs, final = run_scan(rest, prev, taps8, heads8, expand)
    decay = jnp.repeat(jnp.exp(lax.all_gather(cumtot[-1], "ctx")[:, :HEADS]), HEADDIM, axis=1)
    finals = lax.all_gather(final.astype(LOW), "ctx").astype(F32)
    entry = jnp.zeros_like(final)
    for k in range(count - 1):
        entry = jnp.where(k < place, decay[k][None] * entry + finals[k], entry)
    gated_low, mixed, d_gate, d_ssd, acc, d_entry = run_gate(
        y, xbc, gate, cumtot, entry, cotangent, tokens, w_out, rows8, expand
    )
    d_entries = lax.all_gather(d_entry.astype(LOW), "ctx").astype(F32)
    grad_out = mul(gated_low, cotangent, 0, 0)
    grad_gate = mul(normed_low, d_gate, 0, 0)
    d_exit = jnp.zeros_like(d_entry)
    for k in reversed(range(1, count)):
        d_exit = jnp.where(k > place, decay[k][None] * d_exit + d_entries[k], d_exit)
    d_rest, last8, d_prev, conv_acc, head_acc = run_back(
        rest, prev, taps8, heads8, expand, d_ssd, starts, runs, entry, d_exit, rows8
    )
    returned = shifted(d_prev, "ctx", -1)
    d_rest = d_rest.at[block - 8 :, :CONVCH].set((last8 + returned).astype(LOW))
    grad_rest = mul(normed_low, d_rest, 0, 0)
    d_normed = mul(d_gate, w_gate, 1, 1) + mul(d_rest, w_rest, 1, 1)
    d_tokens, d_norm_gain = front_pull(d_normed)
    tokens_grad = cotangent.astype(F32) + d_tokens
    grad_vec = jnp.concatenate(
        [
            d_norm_gain,
            acc[0],
            conv_acc[:CONV].T.reshape(-1),
            conv_acc[4],
            head_acc[0, :HEADS],
            head_acc[1, :HEADS],
            jnp.sum(acc[1].reshape(HEADS, HEADDIM), axis=1),
        ]
    )
    return mixed, tokens_grad, grad_out, grad_gate, grad_rest, grad_vec


def per_device(
    tokens,
    cotangent,
    in_master,
    in_moment,
    in_second,
    out_master,
    out_moment,
    out_second,
    vec_master,
    vec_moment,
    vec_second,
):
    packed = gathered(vec_master).astype(F32)
    tail = jnp.pad(in_master[:, INNER:], ((0, 0), (0, LANES - HEADS)))
    w_rest = gathered(tail)
    w_gate = gathered(in_master[:, :INNER])
    w_out = gathered(out_master)
    results = [
        one_sequence(tokens[b], cotangent[b], w_gate, w_rest, w_out, packed)
        for b in range(tokens.shape[0])
    ]
    mixed = jnp.stack([r[0] for r in results])
    tokens_grad = jnp.stack([r[1] for r in results])
    grad_out, grad_gate, grad_rest, grad_vec = (
        sum(r[k] for r in results) for k in range(2, 6)
    )
    own_out = summed(grad_out)
    own_gate = summed(grad_gate)
    own_rest = summed(grad_rest)[:, : CONVCH + HEADS]
    own_in = jnp.concatenate([own_gate, own_rest], axis=1)
    full_vec = lax.psum(grad_vec, ("dp", "ctx"))
    squares = lax.psum(jnp.sum(own_in * own_in) + jnp.sum(own_out * own_out), "ctx")
    squares = squares + jnp.sum(full_vec * full_vec)
    own_vec = lax.dynamic_slice_in_dim(
        full_vec, lax.axis_index("ctx") * vec_master.shape[0], vec_master.shape[0], 0
    )
    grad_norm = jnp.sqrt(squares)
    factor = 1.0 / jnp.maximum(grad_norm, 1.0)
    in_first, in_square, in_updated = adamw(
        in_master, in_moment, in_second, own_in * factor, 0.05, 0.01
    )
    out_first, out_square, out_updated = adamw(
        out_master, out_moment, out_second, own_out * factor, 0.05, 0.01
    )
    vec_first, vec_square, vec_updated = adamw(
        vec_master, vec_moment, vec_second, own_vec * factor, 0.5, 0.0
    )
    return (
        mixed,
        tokens_grad,
        in_first,
        in_square,
        in_updated,
        out_first,
        out_square,
        out_updated,
        vec_first,
        vec_square,
        vec_updated,
        grad_norm,
    )


def solution(mesh):
    in_specs = (
        P("dp", "ctx", None),
        P("dp", "ctx", None),
        P("ctx", None),
        P("ctx", None),
        P("ctx", None),
        P("ctx", None),
        P("ctx", None),
        P("ctx", None),
        P("ctx"),
        P("ctx"),
        P("ctx"),
    )
    out_specs = (
        P("dp", "ctx", None),
        P("dp", "ctx", None),
        P("ctx", None),
        P("ctx", None),
        P("ctx", None),
        P("ctx", None),
        P("ctx", None),
        P("ctx", None),
        P("ctx"),
        P("ctx"),
        P("ctx"),
        P(),
    )
    return jax.shard_map(
        per_device, mesh=mesh, in_specs=in_specs, out_specs=out_specs, check_vma=False
    )
```

```python
import jax
import jax.numpy as jnp
from jax import lax
from jax.experimental import pallas as pl
from jax.experimental.pallas import tpu as pltpu
from jax.sharding import PartitionSpec as P

D = 768
HEADS = 24
HEADDIM = 64
STATE = 128
CONV = 4
SPAN = 256
STEP = 10
INNER = 1536
CONVCH = 1792
LANES = 128
REST = CONVCH + LANES
PAIRS = HEADS // 2

EPS_NORM = 1e-05
BETA_ONE = 0.9
BETA_TWO = 0.999
ADAM_EPS = 1e-08
HIGH = lax.Precision.HIGHEST
LOW = jnp.bfloat16
F32 = jnp.float32


def mul(a, b, ca=1, cb=0):
    return lax.dot_general(
        a.astype(LOW), b.astype(LOW), (((ca,), (cb,)), ((), ())), preferred_element_type=F32
    )


def spread(v, expand):
    top = v.astype(LOW)
    rest = (v - top.astype(F32)).astype(LOW)
    return mul(top, expand) + mul(rest, expand)


def lower_mask():
    rows = lax.broadcasted_iota(jnp.int32, (SPAN, SPAN), 0)
    cols = lax.broadcasted_iota(jnp.int32, (SPAN, SPAN), 1)
    return rows >= cols


def softplus(z):
    return jnp.maximum(z, 0.0) + jnp.log1p(jnp.exp(-jnp.abs(z)))


def conv_total(ext, taps):
    total = taps[4:5, :] + ext[5 : 5 + SPAN] * taps[0:1, :]
    for k in range(1, CONV):
        total = total + ext[5 + k : 5 + k + SPAN] * taps[k : k + 1, :]
    return total


def scan_kernel(
    rest, prev, taps, heads, expand, y, xbc, cumtot, starts, runs, final, state, tail, run
):
    i = pl.program_id(0)

    @pl.when(i == 0)
    def _():
        state[...] = jnp.zeros_like(state)
        run[...] = jnp.zeros_like(run)
        tail[...] = prev[...]

    ext = jnp.concatenate([tail[...], rest[:, :CONVCH]], axis=0)
    total = conv_total(ext, taps)
    tail[...] = rest[SPAN - 8 :, :CONVCH]
    out = total * jax.nn.sigmoid(total)
    xbc[...] = out.astype(LOW)
    x = out[:, :INNER]
    bmat = out[:, INNER : INNER + STATE].astype(LOW)
    cmat = out[:, INNER + STATE :].astype(LOW)
    step = softplus(rest[:, CONVCH:] + heads[0:1, :])
    logdec = -step * heads[1:2, :]
    lower = lower_mask()
    cum = jnp.dot(
        jnp.where(lower, 1.0, 0.0).astype(F32), logdec, precision=HIGH, preferred_element_type=F32
    )
    cum_t = cum.T
    last = cum[SPAN - 1 :, :]
    before = run[...]
    cumtot[...] = cum + before[0:1, :]
    runs[0] = before
    run[...] = before + last
    e = expand[...]
    xs = (x * spread(step, e)).astype(LOW)
    own = mul(bmat, x * spread(step * jnp.exp(last - cum), e), 0, 0)
    held = state[...]
    starts[0] = held
    inner = mul(cmat, bmat, 1, 1)
    lane = lax.broadcasted_iota(jnp.int32, (SPAN, 2 * HEADDIM), 1) < HEADDIM
    carried = spread(jnp.exp(cum), e) * mul(cmat, held)
    zero = jnp.zeros((), LOW)
    for p in range(PAIRS):
        at = slice(p * 2 * HEADDIM, (p + 1) * 2 * HEADDIM)
        both = carried[:, at]
        for j in range(2):
            h = 2 * p + j
            gap = cum[:, h : h + 1] - cum_t[h : h + 1, :]
            m = (jnp.where(lower, jnp.exp(gap), 0.0) * inner).astype(LOW)
            mine = lane if j == 0 else jnp.logical_not(lane)
            both = both + mul(m, jnp.where(mine, xs[:, at], zero))
        y[:, at] = both
    new = held * spread(jnp.exp(jnp.broadcast_to(last, (8, LANES))), e)[0:1, :] + own
    state[...] = new
    final[...] = new


def gate_kernel(
    y, xbc, gate, cumtot, entry, cot, tokens, w_out, rows, expand,
    gated, mixed, dgate, dssd, acc, dentry,
):
    i = pl.program_id(0)

    @pl.when(i == 0)
    def _():
        acc[...] = jnp.zeros_like(acc)
        dentry[...] = jnp.zeros_like(dentry)

    x = xbc[:, :INNER].astype(F32)
    cmat = xbc[:, INNER + STATE :]
    grown = spread(jnp.exp(cumtot[...]), expand[...])
    gain = rows[0:1, :]
    joined = y[...] + grown * mul(cmat, entry[...]) + rows[1:2, :] * x
    g = gate[...]
    sg = jax.nn.sigmoid(g)
    s = g * sg
    u = joined * s
    r = lax.rsqrt(jnp.mean(u * u, axis=1, keepdims=True) + EPS_NORM)
    n = u * r
    low = (n * gain).astype(LOW)
    gated[...] = low
    w = w_out[...]
    mixed[...] = (tokens[...].astype(F32) + mul(low, w)).astype(LOW)
    dgn = mul(cot[...], w, 1, 1)
    acc[0:1, :] += jnp.sum(dgn * n, axis=0, keepdims=True)
    dn = dgn * gain
    du = r * (dn - n * jnp.mean(dn * n, axis=1, keepdims=True))
    dj = du * s
    dgate[...] = (du * joined * (sg * (1.0 + g * (1.0 - sg)))).astype(LOW)
    dssd[...] = dj.astype(LOW)
    acc[1:2, :] += jnp.sum(dj * x, axis=0, keepdims=True)
    dentry[...] += mul(cmat, grown * dj, 0, 0)


def back_kernel(
    rest, ahead, prev, taps, heads, expand, dssd, starts, runs, entry, d_exit, skip,
    d_rest, last8, d_prev, acc, hacc, adj, nxt, dxs_ref, cb_ref,
):
    i = pl.program_id(0)
    first_span = i == pl.num_programs(0) - 1

    @pl.when(i == 0)
    def _():
        adj[...] = d_exit[...]
        nxt[...] = jnp.zeros_like(nxt)
        acc[...] = jnp.zeros_like(acc)
        hacc[...] = jnp.zeros_like(hacc)

    e = expand[...]
    ext = jnp.concatenate(
        [jnp.where(first_span, prev[...], ahead[:, :CONVCH]), rest[:, :CONVCH]], axis=0
    )
    total = conv_total(ext, taps)
    sig = jax.nn.sigmoid(total)
    out = total * sig
    x = out[:, :INNER]
    bmat = out[:, INNER : INNER + STATE].astype(LOW)
    cmat = out[:, INNER + STATE :].astype(LOW)
    z = rest[:, CONVCH:] + heads[0:1, :]
    step = softplus(z)
    logdec = -step * heads[1:2, :]
    lower = lower_mask()
    tri = jnp.where(lower, 1.0, 0.0).astype(F32)
    cum = jnp.dot(tri, logdec, precision=HIGH, preferred_element_type=F32)
    cum_t = cum.T
    last = cum[SPAN - 1 :, :]
    dy = dssd[...]
    step_e = spread(step, e)
    xs32 = x * step_e
    xs = xs32.astype(LOW)
    g = adj[...]
    span_decay = spread(jnp.exp(jnp.broadcast_to(last, (8, LANES))), e)[0:1, :]
    start = starts[0] + spread(jnp.exp(runs[0]), e)[0:1, :] * entry[...]
    grown = spread(jnp.exp(cum), e)
    tails_e = spread(jnp.exp(last - cum), e)
    dyg = grown * dy.astype(F32)
    from_start = (dyg * mul(cmat, start)).astype(LOW)
    dxs_tail = tails_e * mul(bmat, g)
    to_tail = (xs32 * dxs_tail).astype(LOW)
    grow_sum = mul(from_start, e, 1, 1)
    tail_sum = mul(to_tail, e, 1, 1)
    ends = span_decay * jnp.sum(start * g, axis=0, keepdims=True)
    end_sum = mul(jnp.broadcast_to(ends, (8, INNER)), e, 1, 1)[0:1, :]
    end_sum = end_sum + jnp.sum(tail_sum, axis=0, keepdims=True)
    dc = mul(dyg, start, 1, 1)
    db = mul(xs32 * tails_e, g, 1, 1)
    adj[...] = span_decay * g + mul(cmat, dyg, 0, 0)
    inner = mul(cmat, bmat, 1, 1)
    lane = lax.broadcasted_iota(jnp.int32, (SPAN, 2 * HEADDIM), 1) < HEADDIM
    column = lax.broadcasted_iota(jnp.int32, (SPAN, LANES), 1)
    zero = jnp.zeros((), LOW)
    cb_ref[...] = jnp.zeros_like(cb_ref)
    dcum = grow_sum - tail_sum
    for p in range(PAIRS):
        at = slice(p * 2 * HEADDIM, (p + 1) * 2 * HEADDIM)
        both = dxs_tail[:, at]
        for j in range(2):
            h = 2 * p + j
            gap = cum[:, h : h + 1] - cum_t[h : h + 1, :]
            decay = jnp.where(lower, jnp.exp(gap), 0.0)
            mine = lane if j == 0 else jnp.logical_not(lane)
            part = jnp.where(mine, dy[:, at], zero)
            back = mul(part, xs[:, at], 1, 1) * decay
            cb_ref[...] += back
            both = both + mul(decay * inner, part, 0, 0)
            pull = (back * inner).astype(LOW)
            unit = jnp.where(column == h, 1.0, 0.0).astype(LOW)
            dcum = dcum + (mul(pull, unit) - mul(pull, unit, 0, 0))
        dxs_ref[:, at] = both
    d_inner = cb_ref[...]
    dc = dc + mul(d_inner, bmat)
    db = db + mul(d_inner, cmat, 0, 0)
    dxs = dxs_ref[...]
    d_logdec = end_sum + lax.dot_general(
        tri, dcum, (((0,), (0,)), ((), ())), precision=HIGH, preferred_element_type=F32
    )
    d_step = mul(x * dxs, e, 1, 1) - d_logdec * heads[1:2, :]
    real = column < HEADS
    d_raw = jnp.where(real, d_step * jax.nn.sigmoid(z), 0.0)
    hacc[0:1, :] += jnp.sum(d_raw, axis=0, keepdims=True)
    hacc[1:2, :] += jnp.sum(d_logdec * logdec, axis=0, keepdims=True)
    dx = step_e * dxs + skip[1:2, :] * dy.astype(F32)
    d_out = jnp.concatenate([dx, db, dc], axis=1)
    dt = d_out * (sig * (1.0 + total * (1.0 - sig)))
    for k in range(CONV):
        acc[k : k + 1, :] += jnp.sum(dt * ext[5 + k : 5 + k + SPAN], axis=0, keepdims=True)
    acc[4:5, :] += jnp.sum(dt, axis=0, keepdims=True)
    later = jnp.concatenate([dt, nxt[...]], axis=0)
    d_in = later[:SPAN] * taps[3:4, :]
    for k in range(CONV - 1):
        d_in = d_in + later[3 - k : 3 - k + SPAN] * taps[k : k + 1, :]
    d_rest[:, :CONVCH] = d_in.astype(LOW)
    d_rest[:, CONVCH:] = d_raw.astype(LOW)

    @pl.when(i == 0)
    def _():
        last8[...] = d_in[SPAN - 8 :]

    front = dt[:8]
    nxt[...] = front
    edge = jnp.concatenate([jnp.zeros_like(front), front, jnp.zeros_like(front)], axis=0)
    d_before = edge[:8] * taps[3:4, :]
    for k in range(CONV - 1):
        d_before = d_before + edge[3 - k : 11 - k] * taps[k : k + 1, :]
    d_prev[...] = d_before


def whole(*shape):
    return pl.BlockSpec(shape, lambda i: (0,) * len(shape))


def span(width):
    return pl.BlockSpec((SPAN, width), lambda i: (i, 0))


def params():
    return pltpu.CompilerParams(vmem_limit_bytes=56 * 1024 * 1024)


def shape(dims, kind=F32):
    return jax.ShapeDtypeStruct(dims, kind)


def run_scan(rest, prev, taps, heads, expand):
    rows = rest.shape[0]
    n = rows // SPAN
    return pl.pallas_call(
        scan_kernel,
        grid=(n,),
        in_specs=[
            span(REST), whole(8, CONVCH), whole(8, CONVCH), whole(8, LANES), whole(LANES, INNER),
        ],
        out_specs=[
            span(INNER), span(CONVCH), span(LANES),
            pl.BlockSpec((1, STATE, INNER), lambda i: (i, 0, 0)),
            pl.BlockSpec((1, 8, LANES), lambda i: (i, 0, 0)),
            whole(STATE, INNER),
        ],
        out_shape=[
            shape((rows, INNER)), shape((rows, CONVCH), LOW), shape((rows, LANES)),
            shape((n, STATE, INNER)), shape((n, 8, LANES)), shape((STATE, INNER)),
        ],
        scratch_shapes=[
            pltpu.VMEM((STATE, INNER), F32), pltpu.VMEM((8, CONVCH), F32),
            pltpu.VMEM((8, LANES), F32),
        ],
        compiler_params=params(),
        name="span_scan",
    )(rest, prev, taps, heads, expand)


def run_gate(y, xbc, gate, cumtot, entry, cot, tokens, w_out, rows8, expand):
    rows = y.shape[0]
    return pl.pallas_call(
        gate_kernel,
        grid=(rows // SPAN,),
        in_specs=[
            span(INNER), span(CONVCH), span(INNER), span(LANES), whole(STATE, INNER),
            span(D), span(D), whole(INNER, D), whole(8, INNER), whole(LANES, INNER),
        ],
        out_specs=[
            span(INNER), span(D), span(INNER), span(INNER), whole(8, INNER), whole(STATE, INNER),
        ],
        out_shape=[
            shape((rows, INNER), LOW), shape((rows, D), LOW), shape((rows, INNER), LOW),
            shape((rows, INNER), LOW), shape((8, INNER)), shape((STATE, INNER)),
        ],
        compiler_params=params(),
        name="gate_and_back",
    )(y, xbc, gate, cumtot, entry, cot, tokens, w_out, rows8, expand)


def run_back(rest, prev, taps, heads, expand, dssd, starts, runs, entry, d_exit, rows8):
    rows = rest.shape[0]
    n = rows // SPAN
    flip = lambda i: (n - 1 - i, 0)
    flip3 = lambda i: (n - 1 - i, 0, 0)
    edge = SPAN // 8
    return pl.pallas_call(
        back_kernel,
        grid=(n,),
        in_specs=[
            pl.BlockSpec((SPAN, REST), flip),
            pl.BlockSpec((8, REST), lambda i: (jnp.maximum((n - 1 - i) * edge - 1, 0), 0)),
            whole(8, CONVCH), whole(8, CONVCH), whole(8, LANES), whole(LANES, INNER),
            pl.BlockSpec((SPAN, INNER), flip),
            pl.BlockSpec((1, STATE, INNER), flip3),
            pl.BlockSpec((1, 8, LANES), flip3),
            whole(STATE, INNER), whole(STATE, INNER), whole(8, INNER),
        ],
        out_specs=[
            pl.BlockSpec((SPAN, REST), flip),
            whole(8, CONVCH), whole(8, CONVCH), whole(8, CONVCH), whole(8, LANES),
        ],
        out_shape=[
            shape((rows, REST), LOW), shape((8, CONVCH)), shape((8, CONVCH)),
            shape((8, CONVCH)), shape((8, LANES)),
        ],
        scratch_shapes=[
            pltpu.VMEM((STATE, INNER), F32), pltpu.VMEM((8, CONVCH), F32),
            pltpu.VMEM((SPAN, INNER), F32), pltpu.VMEM((SPAN, SPAN), F32),
        ],
        compiler_params=params(),
        name="span_back",
    )(rest, rest, prev, taps, heads, expand, dssd, starts, runs, entry, d_exit, rows8)


def unpack(packed):
    offset = 0
    pieces = []
    for count in (D, INNER, CONVCH * CONV, CONVCH, HEADS, HEADS, HEADS):
        pieces.append(packed[offset : offset + count])
        offset = offset + count
    return pieces


def rms_scale(values, gain):
    return values * lax.rsqrt(jnp.mean(values * values, axis=-1, keepdims=True) + EPS_NORM) * gain


def shifted(block, axis, distance):
    devices = range(lax.axis_size(axis))
    route = [(i - distance, i) for i in devices if i - distance in devices]
    return lax.ppermute(block, axis, route)


def adamw(master, moment, second, grad, rate, decay):
    first = BETA_ONE * moment + (1.0 - BETA_ONE) * grad
    square = BETA_TWO * second + (1.0 - BETA_TWO) * grad * grad
    ahead = first / (1.0 - BETA_ONE**STEP)
    scale = square / (1.0 - BETA_TWO**STEP)
    updated = master - rate * (ahead / (jnp.sqrt(scale) + ADAM_EPS) + decay * master)
    return (first, square, updated)


def crossed(block, distance):
    count = lax.axis_size("ctx")
    return lax.ppermute(block, "ctx", [(i, i ^ distance) for i in range(count)])


def gathered(shard):
    place = lax.axis_index("ctx")
    upper, odd = place // 2 == 1, place % 2 == 1
    far = crossed(shard, 2)
    mine = jnp.stack([jnp.where(upper, far, shard), jnp.where(upper, shard, far)])
    near = crossed(mine, 1)
    both = jnp.stack([jnp.where(odd, near, mine), jnp.where(odd, mine, near)], axis=1)
    return both.reshape((-1,) + shard.shape[1:])


def scattered(grad):
    place = lax.axis_index("ctx")
    upper, odd = place // 2 == 1, place % 2 == 1
    parts = grad.reshape((2, 2, -1) + grad.shape[1:])
    even_part, odd_part = parts[:, 0], parts[:, 1]
    near = crossed(jnp.where(odd, even_part, odd_part).astype(LOW), 1)
    half = jnp.where(odd, odd_part, even_part) + near.astype(F32)
    far = crossed(jnp.where(upper, half[0], half[1]).astype(LOW), 2)
    return jnp.where(upper, half[1], half[0]) + far.astype(F32)


def offload_scattered(grad):
    return lax.psum_scatter(grad.astype(LOW), "ctx", scatter_dimension=0, tiled=True)


VEC_COLS = slice(CONVCH + HEADS, CONVCH + HEADS + 15)


def stack8(*rows):
    out = jnp.stack(rows)
    return jnp.pad(out, ((0, 8 - out.shape[0]), (0, 0)))


def one_sequence(tokens, cotangent, w_gate, w_rest, w_out, packed):
    norm_gain, gate_gain, taps, conv_bias, step_bias, log_rate, skip_gain = unpack(packed)
    place = lax.axis_index("ctx")
    count = lax.axis_size("ctx")
    block = tokens.shape[0]
    flat = tokens.astype(F32)
    normed, front_pull = jax.vjp(rms_scale, flat, norm_gain)
    normed_low = normed.astype(LOW)
    rest = jnp.dot(normed_low, w_rest, preferred_element_type=F32)
    prev = shifted(rest[block - 8 :, :CONVCH], "ctx", 1)
    gate = jnp.dot(normed_low, w_gate, preferred_element_type=F32)
    taps8 = jnp.pad(
        jnp.concatenate([taps.reshape(CONVCH, CONV).T, conv_bias[None]]), ((0, 3), (0, 0))
    )
    heads8 = jnp.pad(stack8(step_bias, jnp.exp(log_rate)), ((0, 0), (0, LANES - HEADS)))
    rows8 = stack8(gate_gain, jnp.repeat(skip_gain, HEADDIM))
    expand = (jnp.arange(LANES)[:, None] == jnp.arange(INNER)[None, :] // HEADDIM).astype(LOW)
    y, xbc, cumtot, starts, runs, final = run_scan(rest, prev, taps8, heads8, expand)
    decay = jnp.repeat(jnp.exp(lax.all_gather(cumtot[-1], "ctx")[:, :HEADS]), HEADDIM, axis=1)
    finals = lax.all_gather(final.astype(LOW), "ctx").astype(F32)
    entry = jnp.zeros_like(final)
    for k in range(count - 1):
        entry = jnp.where(k < place, decay[k][None] * entry + finals[k], entry)
    gated_low, mixed, d_gate, d_ssd, acc, d_entry = run_gate(
        y, xbc, gate, cumtot, entry, cotangent, tokens, w_out, rows8, expand
    )
    d_entries = lax.all_gather(d_entry.astype(LOW), "ctx").astype(F32)
    grad_out = mul(gated_low, cotangent, 0, 0)
    grad_gate = mul(normed_low, d_gate, 0, 0)
    d_exit = jnp.zeros_like(d_entry)
    for k in reversed(range(1, count)):
        d_exit = jnp.where(k > place, decay[k][None] * d_exit + d_entries[k], d_exit)
    d_rest, last8, d_prev, conv_acc, head_acc = run_back(
        rest, prev, taps8, heads8, expand, d_ssd, starts, runs, entry, d_exit, rows8
    )
    returned = shifted(d_prev, "ctx", -1)
    d_rest = d_rest.at[block - 8 :, :CONVCH].set((last8 + returned).astype(LOW))
    grad_rest = mul(normed_low, d_rest, 0, 0)
    d_normed = mul(d_gate, w_gate, 1, 1) + mul(d_rest, w_rest, 1, 1)
    d_tokens, d_norm_gain = front_pull(d_normed)
    tokens_grad = cotangent.astype(F32) + d_tokens
    grad_vec = jnp.concatenate(
        [
            d_norm_gain,
            acc[0],
            conv_acc[:CONV].T.reshape(-1),
            conv_acc[4],
            head_acc[0, :HEADS],
            head_acc[1, :HEADS],
            jnp.sum(acc[1].reshape(HEADS, HEADDIM), axis=1),
        ]
    )
    return mixed, tokens_grad, grad_out, grad_gate, grad_rest, grad_vec


def per_device(
    tokens,
    cotangent,
    in_master,
    in_moment,
    in_second,
    out_master,
    out_moment,
    out_second,
    vec_master,
    vec_moment,
    vec_second,
):
    rows, chunk = in_master.shape[0], vec_master.shape[0]
    columns = VEC_COLS.stop - VEC_COLS.start
    spare = jnp.pad(vec_master, (0, rows * columns - chunk)).reshape(rows, columns)
    tail = jnp.concatenate([in_master[:, INNER:], spare], axis=1)
    tail = jnp.pad(tail, ((0, 0), (0, REST - VEC_COLS.stop))).astype(LOW)
    w_rest = gathered(tail)
    packed = w_rest[:, VEC_COLS].reshape(-1, rows * columns)[:, :chunk].reshape(-1).astype(F32)
    w_gate = gathered(in_master[:, :INNER].astype(LOW))
    w_out = gathered(out_master.astype(LOW))
    results = [
        one_sequence(tokens[b], cotangent[b], w_gate, w_rest, w_out, packed)
        for b in range(tokens.shape[0])
    ]
    mixed = jnp.stack([r[0] for r in results])
    tokens_grad = jnp.stack([r[1] for r in results])
    grad_out, grad_gate, grad_rest, grad_vec = (
        sum(r[k] for r in results) for k in range(2, 6)
    )
    early = lax.psum((offload_scattered(grad_out), offload_scattered(grad_gate)), "dp")
    vec_rows = jnp.pad(grad_vec.reshape(-1, chunk), ((0, 0), (0, rows * columns - chunk)))
    vec_rows = vec_rows.reshape(-1, columns)
    grad_rest = grad_rest + jnp.pad(
        vec_rows, ((0, 0), (VEC_COLS.start, REST - VEC_COLS.stop))
    )
    late = scattered(grad_rest).astype(LOW)
    early, late = lax.optimization_barrier((early, late))
    own_out, own_gate = (part.astype(F32) for part in early)
    own_rest = lax.psum(late, "dp").astype(F32)
    own_in = jnp.concatenate([own_gate, own_rest[:, : CONVCH + HEADS]], axis=1)
    own_vec = own_rest[:, VEC_COLS].reshape(-1)[:chunk]
    squares = lax.psum(
        jnp.sum(own_gate * own_gate) + jnp.sum(own_rest * own_rest) + jnp.sum(own_out * own_out),
        "ctx",
    )
    grad_norm = jnp.sqrt(squares)
    factor = 1.0 / jnp.maximum(grad_norm, 1.0)
    in_first, in_square, in_updated = adamw(
        in_master, in_moment, in_second, own_in * factor, 0.05, 0.01
    )
    out_first, out_square, out_updated = adamw(
        out_master, out_moment, out_second, own_out * factor, 0.05, 0.01
    )
    vec_first, vec_square, vec_updated = adamw(
        vec_master, vec_moment, vec_second, own_vec * factor, 0.5, 0.0
    )
    return (
        mixed,
        tokens_grad,
        in_first,
        in_square,
        in_updated,
        out_first,
        out_square,
        out_updated,
        vec_first,
        vec_square,
        vec_updated,
        grad_norm,
    )


def solution(mesh):
    in_specs = (
        P("dp", "ctx", None),
        P("dp", "ctx", None),
        P("ctx", None),
        P("ctx", None),
        P("ctx", None),
        P("ctx", None),
        P("ctx", None),
        P("ctx", None),
        P("ctx"),
        P("ctx"),
        P("ctx"),
    )
    out_specs = (
        P("dp", "ctx", None),
        P("dp", "ctx", None),
        P("ctx", None),
        P("ctx", None),
        P("ctx", None),
        P("ctx", None),
        P("ctx", None),
        P("ctx", None),
        P("ctx"),
        P("ctx"),
        P("ctx"),
        P(),
    )
    return jax.shard_map(
        per_device, mesh=mesh, in_specs=in_specs, out_specs=out_specs, check_vma=False
    )
```
